32 devices in a mesh: grp: 2 (over x), col: 16 (over z, y, core).
Axes of the slice: x: 2, y: 2, z: 4, core: 2. Of those that a mesh axis runs over, the one named last changes fastest.
Arguments:
- leaf_right_hand: float32 [320, 256, 128], P(('grp', 'col')), parts along dimension 0, may hold values from -6 to 6
- leaf_diagonal_inverse: bfloat16 [320, 256, 256], P(('grp', 'col')), parts along dimension 0, as said below
- leaf_coupling: bfloat16 [320, 4, 256, 256], P(('grp', 'col')), parts along dimension 0, may hold values from -0.03125 to 0.03125
- leaf_pattern: int32 [320, 4], P(('grp', 'col')), parts along dimension 0, may hold values 0 or 1
- top_rhs: float32 [32, 256, 128], P(('grp', 'col')), parts along dimension 0, may hold values from -6 to 6
- top_inverse: bfloat16 [32, 256, 256], P(('grp', 'col')), parts along dimension 0, as said below
- top_coupling: bfloat16 [32, 4, 256, 256], P(('grp', 'col')), parts along dimension 0, may hold values from -0.09375 to 0.09375
Outputs:
- leaf_solution: float32 [320, 256, 128], P(('grp', 'col')), parts along dimension 0
- top_solution: float32 [32, 256, 128], P(('grp', 'col')), parts along dimension 0
The draws below stay inside these ranges and needn't reach their ends.
There are 2 independent parts, one for each index of `grp`. The reference program is written for one: setup_inputs(seed, part) draws one part's arguments, and reference() takes and returns one part's arrays. A program takes and returns all parts, laid end to end along the dimension named above; each array names one. Nothing has to cross between parts.
Inputs may be any that keep to these rules, and one draw needn't show every extreme that they name: `leaf_diagonal_inverse`: lower triangular, diagonal between 0.7 and 1.3. `top_inverse`: lower triangular, diagonal between 0.7 and 1.3.
All inputs are finite; a program needn't handle non-finite values. No bound on the sum of `leaf_pattern` on one device may be relied on, other than what follows from the above.
Results may differ from the reference program's by a relative error of at most 0.0044.
Values sent between devices are 32-bit elements; how exact they have to be, the bound alone decides.
A program may use at most 64 MiB of HBM per device.

```python
import math
import jax
import jax.numpy as jnp
import numpy as np
from jax import lax

SN_WIDTH = 256
RHS = 128
LEAVES = 10
LEVELS = 4
N_COL = 16


def triangle(diag_key, lower, blocks, width):
    rows = lax.broadcasted_iota(jnp.int32, (width, width), 0)
    cols = lax.broadcasted_iota(jnp.int32, (width, width), 1)
    diagonal = jax.random.uniform(diag_key, (blocks, width, 1), jnp.float32, 0.7, 1.3)
    result = jnp.where(rows > cols, lower, 0.0) + jnp.where(rows == cols, diagonal, 0.0)
    return result.astype(jnp.bfloat16)


def draw_leaf_diagonal_inverse(key, part):
    diag_key = jax.random.fold_in(key, 11)
    low_key = jax.random.fold_in(key, 12)
    shape = (N_COL * LEAVES, SN_WIDTH, SN_WIDTH)
    lower = jax.random.truncated_normal(low_key, -4.0, 4.0, shape, jnp.float32) * (0.6 / math.sqrt(SN_WIDTH))
    return triangle(diag_key, lower, N_COL * LEAVES, SN_WIDTH)


def draw_top_inverse(key, part):
    diag_key = jax.random.fold_in(key, 21)
    low_key = jax.random.fold_in(key, 22)
    shape = (N_COL, SN_WIDTH, SN_WIDTH)
    lower = jax.random.truncated_normal(low_key, -4.0, 4.0, shape, jnp.float32) * (0.6 / math.sqrt(SN_WIDTH))
    return triangle(diag_key, lower, N_COL, SN_WIDTH)


def with_ends(array, rng, least, top_value):
    shape = array.shape
    place = [jax.random.randint(jax.random.fold_in(rng, axis), (), 0, shape[axis]) for axis in range(len(shape))]
    array = array.at[tuple(place)].set(least)
    longest = shape.index(max(shape))
    place[longest] = (place[longest] + 1) % shape[longest]
    return array.at[tuple(place)].set(top_value)


def steps_of(rng, extent, split, low, high):
    gain, own = 1.0, jax.random.fold_in(rng, 6)
    for dim, shards_of in split:
        steps = jnp.exp(jax.random.uniform(jax.random.fold_in(own, dim), (shards_of,), jnp.float32, low / len(split), high / len(split)))
        gain = gain * jnp.repeat(steps, extent[dim] // shards_of).reshape([-1 if axis == dim else 1 for axis in range(len(extent))])
    return gain


def gaussian(key, extent, scale, reach, split=(), kind=jnp.bfloat16):
    array = jax.random.normal(key, extent, jnp.float32) * scale
    if len(split) > 0:
        array = steps_of(key, extent, split, -0.22, 0.18) * array
    return jnp.clip(array, min=-reach, max=reach).astype(kind)


def setup_inputs(seed: int = 0, part: int = 0) -> dict:
    keys = jax.random.split(jax.random.key(seed), 8)
    own_keys = jax.random.split(jax.random.fold_in(keys[7], part), 8)
    leaf_right_hand = gaussian(own_keys[0], (N_COL * LEAVES, SN_WIDTH, RHS), 1.0, 6.0, ((0, 16),), jnp.float32)
    leaf_diagonal_inverse = draw_leaf_diagonal_inverse(jax.random.fold_in(jax.random.fold_in(keys[7], part), 71), part)
    leaf_coupling = gaussian(own_keys[2], (N_COL * LEAVES, LEVELS, SN_WIDTH, SN_WIDTH), (SN_WIDTH * LEAVES * N_COL) ** -0.5, 0.03125, ((0, 16),))
    leaf_pattern = with_ends((jax.random.randint(own_keys[3], (N_COL * LEAVES, LEVELS), 0, 4) < 3).astype(jnp.int32), jax.random.fold_in(own_keys[3], 1), 0, 1)
    top_rhs = gaussian(own_keys[4], (N_COL, SN_WIDTH, RHS), 1.0, 6.0, ((0, 16),), jnp.float32)
    top_inverse = draw_top_inverse(jax.random.fold_in(jax.random.fold_in(keys[7], part), 71), part)
    top_coupling = gaussian(own_keys[6], (N_COL, LEVELS, SN_WIDTH, SN_WIDTH), (SN_WIDTH * N_COL) ** -0.5, 0.09375, ((0, 16),))
    return {"leaf_right_hand": leaf_right_hand, "leaf_diagonal_inverse": leaf_diagonal_inverse, "leaf_coupling": leaf_coupling, "leaf_pattern": leaf_pattern, "top_rhs": top_rhs, "top_inverse": top_inverse, "top_coupling": top_coupling}


def random_key(value):
    return lax.optimization_barrier(value.astype(jnp.bfloat16)).astype(jnp.float32)


def leaf_up(inputs):
    right_hand_block, block_inverse, coupling_block, pattern_block = inputs
    forward_sweep = jnp.einsum("efj,ejs->efs", block_inverse.astype(jnp.float32), random_key(right_hand_block))
    masked = pattern_block.astype(jnp.float32)[:, :, None, None] * random_key(forward_sweep)[:, None]
    terms = jnp.einsum("ikab,ikbr->kar", coupling_block.astype(jnp.float32), masked)
    return forward_sweep, terms


def leaf_down(inputs):
    forward_sweep, block_inverse, coupling_block, pattern_block, path_block = inputs
    masked = pattern_block.astype(jnp.float32)[:, :, None, None] * random_key(path_block)[None]
    carried_value = jnp.einsum("ikab,ikar->ibr", coupling_block.astype(jnp.float32), masked)
    return jnp.einsum("vdu,vdo->vuo", block_inverse.astype(jnp.float32), random_key(forward_sweep - carried_value))


def reference(leaf_right_hand, leaf_diagonal_inverse, leaf_coupling, leaf_pattern, top_rhs, top_inverse, top_coupling):
    count = N_COL
    depth = LEVELS
    shaped_rhs = leaf_right_hand.reshape(count, LEAVES, SN_WIDTH, RHS)
    shaped_inverse = leaf_diagonal_inverse.reshape(count, LEAVES, SN_WIDTH, SN_WIDTH)
    shaped_coupling = leaf_coupling.reshape(count, LEAVES, depth, SN_WIDTH, SN_WIDTH)
    shaped_pattern = leaf_pattern.reshape(count, LEAVES, depth)
    leaf_forward, leaf_terms = lax.map(leaf_up, (shaped_rhs, shaped_inverse, shaped_coupling, shaped_pattern))
    top_terms = jnp.zeros((count, depth, SN_WIDTH, RHS), jnp.float32)
    top_forward = jnp.zeros((count, SN_WIDTH, RHS), jnp.float32)
    for level in reversed(range(depth)):
        group = 2 ** (depth - level)
        owners = np.arange(2 ** level) * group + group // 2 - 1
        gathered = (leaf_terms[:, level] + top_terms[:, level]).reshape(2 ** level, group, SN_WIDTH, RHS).sum(axis=1)
        solved = jnp.einsum("nab,nbr->nar", top_inverse[owners].astype(jnp.float32), random_key(top_rhs[owners] - gathered))
        top_forward = top_forward.at[owners].set(solved)
        if level > 0:
            upward = jnp.einsum("nkab,nbr->nkar", top_coupling[owners, :level].astype(jnp.float32), random_key(solved))
            top_terms = top_terms.at[owners, :level].set(upward)
    path_values = jnp.zeros((count, depth, SN_WIDTH, RHS), jnp.float32)
    top_solution = jnp.zeros((count, SN_WIDTH, RHS), jnp.float32)
    for level in range(depth):
        group = 2 ** (depth - level)
        owners = np.arange(2 ** level) * group + group // 2 - 1
        base = top_forward[owners]
        if level > 0:
            known = path_values[owners, :level]
            carried_value = jnp.einsum("nkab,nkar->nbr", top_coupling[owners, :level].astype(jnp.float32), random_key(known))
            base = base - carried_value
        solved = jnp.einsum("nab,nar->nbr", top_inverse[owners].astype(jnp.float32), random_key(base))
        top_solution = top_solution.at[owners].set(solved)
        path_values = path_values.at[:, level].set(jnp.repeat(solved, group, axis=0))
    top_solution = top_solution.at[count - 1].set(path_values[count - 1, 0])
    leaf_solution = lax.map(leaf_down, (leaf_forward, shaped_inverse, shaped_coupling, shaped_pattern, path_values))
    return leaf_solution.reshape(count * LEAVES, SN_WIDTH, RHS), top_solution
```

```python
import functools

import jax
import jax.numpy as jnp
from jax import lax
from jax.experimental import pallas as pl
from jax.experimental.pallas import tpu as pltpu
from jax.sharding import PartitionSpec as P

F32, BF16 = jnp.float32, jnp.bfloat16


def mm(a, b):
    return jnp.dot(a.astype(BF16), b.astype(BF16), preferred_element_type=F32)


def kernel(
    depth,
    rhs_hbm, dinv_hbm, coup_hbm, pat, trhs_hbm, tinv_hbm, tcoup_hbm,
    sol_hbm, top_hbm,
    rhs, dinv, coup, trhs, tinv, tcoup, fwd, fwd_t, out, top_out,
    terms, slots, stage, anc, path, own_x, y_t,
    in_sem, coup_sem, tin_sem, out_sem, top_sem,
    slot_sem, anc_sem, path_sem, part_send, up_send, down_send,
):
    leaves = rhs.shape[0]
    last = depth - 1
    me = lax.axis_index("col")
    even = lax.rem(me, 2) == 0
    odd = lax.rem(me, 2) == 1
    partner = jnp.where(even, me + 1, me - 1)

    def node(level):
        half = 1 << (last - level)
        is_node = lax.rem(me, 2 * half) == half - 1
        left = lax.rem((me + 1 - half) // (2 * half), 2) == 0
        parent = jnp.where(left, me + half, me - half)
        return is_node, left, parent, half // 2

    def load(src, dst, sem):
        return pltpu.make_async_copy(src, dst, sem)

    copy_rhs = load(rhs_hbm, rhs, in_sem.at[0])
    copy_dinv = load(dinv_hbm, dinv, in_sem.at[1])
    copy_coup = [load(coup_hbm.at[:, k], coup.at[:, k], coup_sem.at[k]) for k in range(depth)]
    copy_tinv = load(tinv_hbm, tinv, tin_sem.at[0])
    copy_trhs = load(trhs_hbm, trhs, tin_sem.at[1])
    copy_tcoup = load(tcoup_hbm, tcoup, tin_sem.at[2])
    copy_dinv.start()
    copy_rhs.start()
    copy_coup[last].start()
    copy_tinv.start()
    copy_trhs.start()
    for k in reversed(range(last)):
        copy_coup[k].start()
    copy_tcoup.start()

    barrier = pltpu.get_barrier_semaphore()

    def greet(device):
        pl.semaphore_signal(barrier, inc=1, device_id={"col": device}, device_id_type=pl.DeviceIdType.MESH)

    greet(partner)
    for level in range(depth):
        is_node, left, parent, quarter = node(level)

        @pl.when(is_node)
        def _():
            if level > 0:
                greet(parent)
            if level < last:
                greet(me - quarter)
                greet(me + quarter)

    def send(src, dst, send_sem, recv_sem, device):
        return pltpu.make_async_remote_copy(
            src_ref=src, dst_ref=dst, send_sem=send_sem, recv_sem=recv_sem,
            device_id={"col": device}, device_id_type=pl.DeviceIdType.MESH,
        )

    def part_copy(k):
        return send(terms.at[k], slots.at[0, k], part_send.at[k], slot_sem.at[0, k], partner)

    def up_copy(side, k, parent):
        return send(stage.at[k], slots.at[side, k], up_send.at[k], slot_sem.at[side, k], parent)

    def down_copy(src, side, k, child, to_even):
        dst, sem = (path, path_sem) if to_even else (anc, anc_sem)
        return send(src, dst.at[k], down_send.at[side, k], sem.at[k], child)

    def pair_copy(k):
        return send(path.at[k], path.at[k], down_send.at[0, k], path_sem.at[k], partner)

    def slot_wait(side, k):
        send(slots.at[side, k], slots.at[side, k], part_send.at[k], slot_sem.at[side, k], partner).wait_recv()

    def anc_wait(k):
        send(anc.at[k], anc.at[k], part_send.at[k], anc_sem.at[k], partner).wait_recv()

    def path_wait(k):
        send(path.at[k], path.at[k], part_send.at[k], path_sem.at[k], partner).wait_recv()

    copy_dinv.wait()
    copy_rhs.wait()
    unroll = max(u for u in range(1, 6) if leaves % u == 0)

    def over_leaves(body):
        def block(b, carry):
            for u in range(unroll):
                body(b * unroll + u)
            return carry
        lax.fori_loop(0, leaves // unroll, block, 0)

    def leaf_solve(i):
        fwd[i] = mm(dinv[i], rhs[i])

    over_leaves(leaf_solve)

    def leaf_term(k):
        copy_coup[k].wait()

        def block(b, acc):
            for u in range(unroll):
                i = b * unroll + u
                acc = acc + pat[i, k].astype(F32) * mm(coup[i, k], fwd[i])
            return acc

        terms[k] = lax.fori_loop(0, leaves // unroll, block, jnp.zeros(terms.shape[1:], F32))

    def flip(i):
        fwd_t[i] = fwd[i].T

    leaf_term(last)
    count = 1
    for level in range(depth):
        is_node = node(level)[0]
        mine = (1 if level > 0 else 0) + (2 if level < last else 0)
        count = count + jnp.where(is_node, mine, 0)
    pl.semaphore_wait(barrier, count)

    @pl.when(odd)
    def _():
        part_copy(last).start()

    for k in reversed(range(last)):
        leaf_term(k)

        @pl.when(odd)
        def _():
            part_copy(k).start()

    copy_tinv.wait()
    copy_trhs.wait()
    copy_tcoup.wait()

    @pl.when(odd)
    def _():
        over_leaves(flip)

    for level in reversed(range(depth)):
        is_node, left, parent, quarter = node(level)

        @pl.when(is_node)
        def _():
            def rest(k):
                slot_wait(0, k)
                if level == last:
                    return terms[k] + slots[0, k]
                slot_wait(1, k)
                return slots[0, k] + slots[1, k]

            y = mm(tinv[0], trhs[0] - rest(level))
            for k in reversed(range(level)):
                stage[k] = rest(k) + mm(tcoup[0, k], y)

                @pl.when(left)
                def _():
                    up_copy(0, k, parent).start()

                @pl.when(jnp.logical_not(left))
                def _():
                    up_copy(1, k, parent).start()

            y_t[...] = y.T

    @pl.when(even)
    def _():
        over_leaves(flip)

    def leaf_back(k):
        x = path[k].astype(BF16)

        def body(i):
            value = fwd_t[i] - pat[i, k].astype(F32) * mm(x, coup[i, k])
            if k < last:
                fwd_t[i] = value
            else:
                out[i] = mm(value, dinv[i]).T
                pltpu.make_async_copy(out.at[i], sol_hbm.at[i], out_sem.at[i]).start()

        over_leaves(body)

    for level in range(last):
        is_node, left, parent, quarter = node(level)

        @pl.when(is_node)
        def _():
            value = y_t[...]
            to_even = level + 1 == last
            for k in range(level):
                anc_wait(k)
                down_copy(anc.at[k], 0, k, me - quarter, to_even).start()
                down_copy(anc.at[k], 1, k, me + quarter, to_even).start()
                value = value - mm(anc[k], tcoup[0, k])
            own_x[...] = mm(value, tinv[0])
            down_copy(own_x, 0, level, me - quarter, to_even).start()
            down_copy(own_x, 1, level, me + quarter, to_even).start()
            top_out[0] = own_x[...].T

    @pl.when(even)
    def _():
        for k in range(last):
            path_wait(k)
            pair_copy(k).start()
            y_t[...] = y_t[...] - mm(path[k], tcoup[0, k])
            if k + 1 == last:
                path[last] = mm(y_t[...], tinv[0])
                pair_copy(last).start()
            leaf_back(k)
        top_out[0] = path[last].T

    @pl.when(odd)
    def _():
        for k in range(last):
            path_wait(k)
            leaf_back(k)
        path_wait(last)

    @pl.when(me == (1 << depth) - 1)
    def _():
        top_out[0] = path[0].T

    copy_top = pltpu.make_async_copy(top_out, top_hbm, top_sem)
    copy_top.start()
    leaf_back(last)

    @pl.when(odd)
    def _():
        for k in range(depth):
            part_copy(k).wait_send()

    for level in range(depth):
        is_node, left, parent, quarter = node(level)

        @pl.when(is_node)
        def _():
            for k in range(level):
                up_copy(0, k, parent).wait_send()
            if level < last:
                for k in range(level + 1):
                    down_copy(own_x, 0, k, partner, True).wait_send()
                    down_copy(own_x, 1, k, partner, True).wait_send()
            else:
                for k in range(depth):
                    pair_copy(k).wait_send()

    copy_top.wait()

    def out_wait(i):
        pltpu.make_async_copy(out.at[i], sol_hbm.at[i], out_sem.at[i]).wait()

    over_leaves(out_wait)


def local(leaf_right_hand, leaf_diagonal_inverse, leaf_coupling, leaf_pattern, top_rhs, top_inverse, top_coupling):
    depth = lax.axis_size("col").bit_length() - 1
    leaves, width, right = leaf_right_hand.shape
    tall, flat = (width, right), (right, width)
    anywhere = pl.BlockSpec(memory_space=pl.ANY)
    sem = pltpu.SemaphoreType.DMA
    return pl.pallas_call(
        functools.partial(kernel, depth),
        out_shape=(
            jax.ShapeDtypeStruct(leaf_right_hand.shape, F32),
            jax.ShapeDtypeStruct(top_rhs.shape, F32),
        ),
        in_specs=[anywhere] * 3 + [pl.BlockSpec(memory_space=pltpu.SMEM)] + [anywhere] * 3,
        out_specs=(anywhere, anywhere),
        scratch_shapes=[
            pltpu.VMEM(leaf_right_hand.shape, F32),
            pltpu.VMEM(leaf_diagonal_inverse.shape, BF16),
            pltpu.VMEM(leaf_coupling.shape, BF16),
            pltpu.VMEM(top_rhs.shape, F32),
            pltpu.VMEM(top_inverse.shape, BF16),
            pltpu.VMEM(top_coupling.shape, BF16),
            pltpu.VMEM((leaves, *tall), F32),
            pltpu.VMEM((leaves, *flat), F32),
            pltpu.VMEM((leaves, *tall), F32),
            pltpu.VMEM((1, *tall), F32),
            pltpu.VMEM((depth, *tall), F32),
            pltpu.VMEM((2, depth, *tall), F32),
            pltpu.VMEM((depth, *tall), F32),
            pltpu.VMEM((depth, *flat), F32),
            pltpu.VMEM((depth, *flat), F32),
            pltpu.VMEM(flat, F32),
            pltpu.VMEM(flat, F32),
            sem((2,)), sem((depth,)), sem((3,)), sem((leaves,)), sem,
            sem((2, depth)), sem((depth,)), sem((depth,)), sem((depth,)), sem((depth,)), sem((2, depth)),
        ],
        compiler_params=pltpu.CompilerParams(
            collective_id=0, has_side_effects=True, vmem_limit_bytes=56 * 2**20
        ),
    )(leaf_right_hand, leaf_diagonal_inverse, leaf_coupling, leaf_pattern, top_rhs, top_inverse, top_coupling)


def solution(mesh):
    both = ("grp", "col")
    three, four = P(both, None, None), P(both, None, None, None)
    in_specs = (three, three, four, P(both, None), three, three, four)
    return jax.shard_map(local, mesh=mesh, in_specs=in_specs, out_specs=(three, three), check_vma=False)
```

```python
import functools

import jax
import jax.numpy as jnp
from jax import lax
from jax.experimental import pallas as pl
from jax.experimental.pallas import tpu as pltpu
from jax.sharding import PartitionSpec as P

F32, BF16 = jnp.float32, jnp.bfloat16


def mm(a, b):
    return jnp.dot(a.astype(BF16), b.astype(BF16), preferred_element_type=F32)


def kernel(
    depth,
    rhs_hbm, dinv_hbm, coup_hbm, pat, trhs_hbm, tinv_hbm, tcoup_hbm,
    sol_hbm, top_hbm,
    rhs, dinv, coup, trhs, tinv, tcoup, fwd, fwd_t, out, top_out,
    terms, slots, stage, path, y_t,
    own_mats, mats, high_rhs, mine, theirs, high_y, high_x,
    in_sem, coup_sem, tin_sem, out_sem, top_sem,
    slot_sem, path_sem, part_send, up_send, down_send,
    mat_send, mat_sem, rhs_sem, swap_send, swap_sem,
):
    leaves = rhs.shape[0]
    last = depth - 1
    hub_level = depth - 2
    me = lax.axis_index("col")
    even = lax.rem(me, 2) == 0
    odd = lax.rem(me, 2) == 1
    partner = jnp.where(even, me + 1, me - 1)
    is_hub = lax.rem(me, 4) == 1
    left = lax.rem(me, 4) == 0
    parent = jnp.where(left, me + 1, me - 1)

    def owner(level):
        span = 1 << (depth - level)
        return lax.rem(me, span) == span // 2 - 1

    def hubs(level):
        span = 1 << (depth - level)
        return [me + 1 - span // 2 + 4 * t + 1 for t in range(span // 4)]

    def owner_of(level):
        span = 1 << (depth - level)
        return me // span * span + span // 2 - 1

    def opposite(level):
        step = 4 << (hub_level - 1 - level)
        return jnp.where(lax.rem(me // step, 2) == 0, me + step, me - step)

    def load(src, dst, sem):
        return pltpu.make_async_copy(src, dst, sem)

    copy_rhs = load(rhs_hbm, rhs, in_sem.at[0])
    copy_dinv = load(dinv_hbm, dinv, in_sem.at[1])
    copy_coup = [load(coup_hbm.at[:, k], coup.at[:, k], coup_sem.at[k]) for k in range(depth)]
    copy_tinv = load(tinv_hbm, tinv, tin_sem.at[0])
    copy_trhs = load(trhs_hbm, trhs, tin_sem.at[1])
    copy_tcoup = load(tcoup_hbm, tcoup, tin_sem.at[2])
    copy_tinv.start()
    copy_trhs.start()
    copy_tcoup.start()
    copy_dinv.start()
    copy_rhs.start()
    for k in reversed(range(depth)):
        copy_coup[k].start()

    barrier = pltpu.get_barrier_semaphore()

    def greet(device):
        pl.semaphore_signal(barrier, inc=1, device_id={"col": device}, device_id_type=pl.DeviceIdType.MESH)

    greet(partner)

    @pl.when(even)
    def _():
        greet(parent)

    @pl.when(is_hub)
    def _():
        greet(me - 1)
        greet(me + 1)
        for level in range(hub_level):
            greet(owner_of(level))
            greet(opposite(level))

    count = 1 + jnp.where(even, 1, 0) + jnp.where(is_hub, 2 + 2 * hub_level, 0)
    for level in range(hub_level):

        @pl.when(owner(level))
        def _():
            for hub in hubs(level):
                greet(hub)

        count = count + jnp.where(owner(level), 1 << (hub_level - level), 0)

    def send(src, dst, send_sem, recv_sem, device):
        return pltpu.make_async_remote_copy(
            src_ref=src, dst_ref=dst, send_sem=send_sem, recv_sem=recv_sem,
            device_id={"col": device}, device_id_type=pl.DeviceIdType.MESH,
        )

    def part_copy(k):
        return send(terms.at[k], slots.at[0, k], part_send.at[k], slot_sem.at[0, k], partner)

    def up_copy(side, k):
        return send(stage.at[k], slots.at[side, k], up_send.at[k], slot_sem.at[side, k], parent)

    def down_copy(src, side, k, child):
        return send(src, path.at[k], down_send.at[side, k], path_sem.at[k], child)

    def pair_copy(k):
        return send(path.at[k], path.at[k], down_send.at[0, k], path_sem.at[k], partner)

    def swap_copy(level, k):
        return send(mine.at[level, k], theirs.at[level, k], swap_send.at[level, k], swap_sem.at[level, k], opposite(level))

    def mat_copy(level, k, t, hub):
        return send(own_mats.at[k], mats.at[level, k], mat_send.at[t, k], mat_sem.at[level, k], hub)

    def rhs_copy(level, t, hub):
        return send(trhs.at[0], high_rhs.at[level], mat_send.at[t, hub_level], rhs_sem.at[level], hub)

    def slot_wait(side, k):
        send(slots.at[side, k], slots.at[side, k], part_send.at[k], slot_sem.at[side, k], partner).wait_recv()

    def path_wait(k):
        send(path.at[k], path.at[k], part_send.at[k], path_sem.at[k], partner).wait_recv()

    copy_tinv.wait()
    copy_trhs.wait()
    copy_tcoup.wait()
    copy_dinv.wait()
    copy_rhs.wait()
    unroll = max(u for u in range(1, 6) if leaves % u == 0)

    def over_leaves(body):
        def block(b, carry):
            for u in range(unroll):
                body(b * unroll + u)
            return carry
        lax.fori_loop(0, leaves // unroll, block, 0)

    def leaf_solve(i):
        fwd[i] = mm(dinv[i], rhs[i])

    over_leaves(leaf_solve)

    def leaf_term(k):
        copy_coup[k].wait()

        def block(b, acc):
            for u in range(unroll):
                i = b * unroll + u
                acc = acc + pat[k, i].astype(F32) * mm(coup[i, k], fwd[i])
            return acc

        terms[k] = lax.fori_loop(0, leaves // unroll, block, jnp.zeros(terms.shape[1:], F32))

    def flip(i):
        fwd_t[i] = fwd[i].T

    pl.semaphore_wait(barrier, count)

    for level in range(hub_level):

        @pl.when(owner(level))
        def _():
            own_mats[level] = tinv[0].astype(F32)
            for t, hub in enumerate(hubs(level)):
                mat_copy(level, level, t, hub).start()
                rhs_copy(level, t, hub).start()
            for k in reversed(range(level)):
                own_mats[k] = tcoup[0, k].astype(F32)
                for t, hub in enumerate(hubs(level)):
                    mat_copy(level, k, t, hub).start()

    for k in reversed(range(depth)):
        leaf_term(k)

        @pl.when(odd)
        def _():
            part_copy(k).start()

    @pl.when(odd)
    def _():
        over_leaves(flip)

    @pl.when(even)
    def _():
        slot_wait(0, last)
        y = mm(tinv[0], trhs[0] - (terms[last] + slots[0, last]))
        for k in reversed(range(last)):
            slot_wait(0, k)
            stage[k] = terms[k] + slots[0, k] + mm(tcoup[0, k], y)

            @pl.when(left)
            def _():
                up_copy(0, k).start()

            @pl.when(jnp.logical_not(left))
            def _():
                up_copy(1, k).start()

        y_t[...] = y.T
        over_leaves(flip)

    @pl.when(is_hub)
    def _():
        def rest(k):
            slot_wait(0, k)
            slot_wait(1, k)
            return slots[0, k] + slots[1, k]

        y = mm(tinv[0], trhs[0] - rest(hub_level))
        top = hub_level - 1
        for k in reversed(range(hub_level)):
            mine[top, k] = rest(k) + mm(tcoup[0, k], y)
            swap_copy(top, k).start()
        y_t[...] = y.T
        for level in reversed(range(hub_level)):
            for k in reversed(range(level + 1)):
                send(
                    own_mats.at[k], mats.at[level, k], mat_send.at[0, k], mat_sem.at[level, k], partner
                ).wait_recv()
            send(
                trhs.at[0], high_rhs.at[level], mat_send.at[0, hub_level], rhs_sem.at[level], partner
            ).wait_recv()
            swap_copy(level, level).wait_recv()
            y = mm(mats[level, level], high_rhs[level] - (mine[level, level] + theirs[level, level]))
            for k in reversed(range(level)):
                swap_copy(level, k).wait_recv()
                mine[level - 1, k] = mine[level, k] + theirs[level, k] + mm(mats[level, k], y)
                swap_copy(level - 1, k).start()
            high_y[level] = y.T

        for level in range(hub_level + 1):
            own = level == hub_level
            value = y_t[...] if own else high_y[level]
            for k in range(level):
                value = value - mm(high_x[k], tcoup[0, k] if own else mats[level, k])
            high_x[level] = mm(value, tinv[0] if own else mats[level, level])
            down_copy(high_x.at[level], 1, level, me + 1).start()
            down_copy(high_x.at[level], 0, level, me - 1).start()
        top_out[0] = high_x[hub_level].T

    def leaf_back(k):
        x = path[k].astype(BF16)

        def body(i):
            value = fwd_t[i] - pat[k, i].astype(F32) * mm(x, coup[i, k])
            if k < last:
                fwd_t[i] = value
            else:
                out[i] = mm(value, dinv[i]).T
                pltpu.make_async_copy(out.at[i], sol_hbm.at[i], out_sem.at[i]).start()

        over_leaves(body)

    @pl.when(even)
    def _():
        for k in range(last):
            path_wait(k)
            pair_copy(k).start()
            y_t[...] = y_t[...] - mm(path[k], tcoup[0, k])
            if k + 1 == last:
                path[last] = mm(y_t[...], tinv[0])
                pair_copy(last).start()
            leaf_back(k)
        top_out[0] = path[last].T

    @pl.when(odd)
    def _():
        for k in range(last):
            path_wait(k)
            leaf_back(k)
        path_wait(last)

    for level in range(hub_level):

        @pl.when(owner(level))
        def _():
            top_out[0] = path[level].T

    @pl.when(me == (1 << depth) - 1)
    def _():
        top_out[0] = path[0].T

    copy_top = pltpu.make_async_copy(top_out, top_hbm, top_sem)
    copy_top.start()
    leaf_back(last)

    @pl.when(odd)
    def _():
        for k in range(depth):
            part_copy(k).wait_send()

    @pl.when(even)
    def _():
        for k in range(last):
            up_copy(0, k).wait_send()
        for k in range(depth):
            pair_copy(k).wait_send()

    @pl.when(is_hub)
    def _():
        for level in range(hub_level):
            for k in range(level + 1):
                swap_copy(level, k).wait_send()
        for k in range(hub_level + 1):
            down_copy(high_x.at[k], 0, k, partner).wait_send()
            down_copy(high_x.at[k], 1, k, partner).wait_send()

    for level in range(hub_level):

        @pl.when(owner(level))
        def _():
            for t, hub in enumerate(hubs(level)):
                rhs_copy(level, t, hub).wait_send()
                for k in range(level + 1):
                    mat_copy(level, k, t, hub).wait_send()

    copy_top.wait()

    def out_wait(i):
        pltpu.make_async_copy(out.at[i], sol_hbm.at[i], out_sem.at[i]).wait()

    over_leaves(out_wait)


def local(leaf_right_hand, leaf_diagonal_inverse, leaf_coupling, leaf_pattern, top_rhs, top_inverse, top_coupling):
    depth = lax.axis_size("col").bit_length() - 1
    high = depth - 2
    leaves, width, right = leaf_right_hand.shape
    tall, flat = (width, right), (right, width)
    anywhere = pl.BlockSpec(memory_space=pl.ANY)
    sem = pltpu.SemaphoreType.DMA
    return pl.pallas_call(
        functools.partial(kernel, depth),
        out_shape=(
            jax.ShapeDtypeStruct(leaf_right_hand.shape, F32),
            jax.ShapeDtypeStruct(top_rhs.shape, F32),
        ),
        in_specs=[anywhere] * 3 + [pl.BlockSpec(memory_space=pltpu.SMEM)] + [anywhere] * 3,
        out_specs=(anywhere, anywhere),
        scratch_shapes=[
            pltpu.VMEM(leaf_right_hand.shape, F32),
            pltpu.VMEM(leaf_diagonal_inverse.shape, BF16),
            pltpu.VMEM(leaf_coupling.shape, BF16),
            pltpu.VMEM(top_rhs.shape, F32),
            pltpu.VMEM(top_inverse.shape, BF16),
            pltpu.VMEM(top_coupling.shape, BF16),
            pltpu.VMEM((leaves, *tall), F32),
            pltpu.VMEM((leaves, *flat), F32),
            pltpu.VMEM((leaves, *tall), F32),
            pltpu.VMEM((1, *tall), F32),
            pltpu.VMEM((depth, *tall), F32),
            pltpu.VMEM((2, depth, *tall), F32),
            pltpu.VMEM((depth, *tall), F32),
            pltpu.VMEM((depth, *flat), F32),
            pltpu.VMEM(flat, F32),
            pltpu.VMEM((high, width, width), F32),
            pltpu.VMEM((high, high, width, width), F32),
            pltpu.VMEM((high, *tall), F32),
            pltpu.VMEM((high, high, *tall), F32),
            pltpu.VMEM((high, high, *tall), F32),
            pltpu.VMEM((high, *flat), F32),
            pltpu.VMEM((high + 1, *flat), F32),
            sem((2,)), sem((depth,)), sem((3,)), sem((leaves,)), sem,
            sem((2, depth)), sem((depth,)), sem((depth,)), sem((depth,)), sem((2, depth)),
            sem((1 << high, high + 1)), sem((high, high)), sem((high,)), sem((high, high)), sem((high, high)),
        ],
        compiler_params=pltpu.CompilerParams(
            collective_id=0, has_side_effects=True, vmem_limit_bytes=56 * 2**20
        ),
    )(leaf_right_hand, leaf_diagonal_inverse, leaf_coupling, leaf_pattern.T, top_rhs, top_inverse, top_coupling)


def solution(mesh):
    both = ("grp", "col")
    three, four = P(both, None, None), P(both, None, None, None)
    in_specs = (three, three, four, P(both, None), three, three, four)
    return jax.shard_map(local, mesh=mesh, in_specs=in_specs, out_specs=(three, three), check_vma=False)
```

```python
import functools

import jax
import jax.numpy as jnp
from jax import lax
from jax.experimental import pallas as pl
from jax.experimental.pallas import tpu as pltpu
from jax.sharding import PartitionSpec as P

F32, BF16 = jnp.float32, jnp.bfloat16


def mm(a, b):
    return jnp.dot(a.astype(BF16), b.astype(BF16), preferred_element_type=F32)


def kernel(
    depth,
    rhs_hbm, dinv_hbm, coup_hbm, pat, trhs_hbm, tinv_hbm, tcoup_hbm,
    sol_hbm, top_hbm,
    rhs, dinv, coup, trhs, tinv, tcoup, fwd, fwd_t, out, top_out,
    terms, slots, stage, path, y_t,
    own_mats, mats, mine, theirs, high_y, high_x,
    in_sem, coup_sem, tin_sem, out_sem, top_sem,
    slot_sem, path_sem, part_send, up_send, down_send,
    mat_send, mat_sem, tip_sem, swap_send, swap_sem,
):
    leaves = rhs.shape[0]
    last = depth - 1
    hub_level = depth - 2
    half = tinv.shape[1] // 2
    me = lax.axis_index("col")
    even = lax.rem(me, 2) == 0
    odd = lax.rem(me, 2) == 1
    partner = jnp.where(even, me + 1, me - 1)
    is_hub = lax.rem(me, 4) == 1
    left = lax.rem(me, 4) == 0
    parent = jnp.where(left, me + 1, me - 1)

    def owner(level):
        span = 1 << (depth - level)
        return lax.rem(me, span) == span // 2 - 1

    def entry(level):
        span = 1 << (depth - level)
        return me // span * span + span // 2 - 3

    def others(level):
        first = 1 << (depth - level - 3)
        return [(t, me + 4 * (t + 1 - first)) for t in range(2 * first) if t + 1 != first]

    def opposite(level):
        step = 4 << (hub_level - 1 - level)
        return jnp.where(lax.rem(me // step, 2) == 0, me + step, me - step)

    def load(src, dst, sem):
        return pltpu.make_async_copy(src, dst, sem)

    copy_rhs = load(rhs_hbm, rhs, in_sem.at[0])
    copy_dinv = load(dinv_hbm, dinv, in_sem.at[1])
    copy_coup = [load(coup_hbm.at[:, k], coup.at[:, k], coup_sem.at[k]) for k in range(depth)]
    copy_tinv = load(tinv_hbm, tinv, tin_sem.at[0])
    copy_trhs = load(trhs_hbm, trhs, tin_sem.at[1])
    copy_tcoup = load(tcoup_hbm, tcoup, tin_sem.at[2])
    copy_tinv.start()
    copy_trhs.start()
    copy_tcoup.start()
    copy_dinv.start()
    copy_rhs.start()
    for k in reversed(range(depth)):
        copy_coup[k].start()

    barrier = pltpu.get_barrier_semaphore()

    def greet(device):
        pl.semaphore_signal(barrier, inc=1, device_id={"col": device}, device_id_type=pl.DeviceIdType.MESH)

    greet(partner)

    @pl.when(even)
    def _():
        greet(parent)

    @pl.when(is_hub)
    def _():
        greet(me - 1)
        greet(me + 1)
        for level in range(hub_level):
            greet(opposite(level))
            here = me == entry(level)

            @pl.when(here)
            def _():
                greet(me + 2)
                for _t, hub in others(level):
                    greet(hub)

            @pl.when(jnp.logical_not(here))
            def _():
                greet(entry(level))

    count = 1 + jnp.where(even, 1, 0) + jnp.where(is_hub, 2 + hub_level, 0)
    for level in range(hub_level):

        @pl.when(owner(level))
        def _():
            greet(me - 2)

        hub_count = jnp.where(me == entry(level), 1 << (hub_level - level), 1)
        count = count + jnp.where(owner(level), 1, 0) + jnp.where(is_hub, hub_count, 0)

    def send(src, dst, send_sem, recv_sem, device):
        return pltpu.make_async_remote_copy(
            src_ref=src, dst_ref=dst, send_sem=send_sem, recv_sem=recv_sem,
            device_id={"col": device}, device_id_type=pl.DeviceIdType.MESH,
        )

    def part_copy(k):
        return send(terms.at[k], slots.at[0, k], part_send.at[k], slot_sem.at[0, k], partner)

    def up_copy(side, k):
        return send(stage.at[k], slots.at[side, k], up_send.at[k], slot_sem.at[side, k], parent)

    def down_copy(src, side, k, child):
        return send(src, path.at[k], down_send.at[side, k], path_sem.at[k], child)

    def pair_copy(k):
        return send(path.at[k], path.at[k], down_send.at[0, k], path_sem.at[k], partner)

    def swap_copy(level, k):
        return send(mine.at[level, k], theirs.at[level, k], swap_send.at[level, k], swap_sem.at[level, k], opposite(level))

    def mat_parts(src, level, k, t, device):
        dst, sems = mats.at[level, k], mat_send.at[level, t]
        if k < level:
            return [send(src, dst, sems.at[k], mat_sem.at[level, k], device)]
        low, up = pl.ds(half, half), pl.ds(0, half)
        return [
            send(src.at[low], dst.at[low], sems.at[k], mat_sem.at[level, k], device),
            send(src.at[up, up], dst.at[up, up], sems.at[hub_level], tip_sem.at[level], device),
        ]

    def own_parts(level, k):
        return mat_parts(own_mats.at[k], level, k, 0, me - 2)

    def mat_wait(level):
        for k in range(level + 1):
            for copy in mat_parts(mats.at[level, k], level, k, 0, partner):
                copy.wait_recv()

    def slot_wait(side, k):
        send(slots.at[side, k], slots.at[side, k], part_send.at[k], slot_sem.at[side, k], partner).wait_recv()

    def path_wait(k):
        send(path.at[k], path.at[k], part_send.at[k], path_sem.at[k], partner).wait_recv()

    copy_tinv.wait()
    copy_trhs.wait()
    copy_tcoup.wait()
    for level in range(hub_level):
        mats[level, level, :half, half:] = jnp.zeros((half, half), F32)

        @pl.when(owner(level))
        def _():
            for k in range(level + 1):
                own_mats[k] = (tinv[0] if k == level else tcoup[0, k]).astype(F32)

    pl.semaphore_wait(barrier, count)

    for level in range(hub_level):

        @pl.when(owner(level))
        def _():
            for k in reversed(range(level + 1)):
                for copy in own_parts(level, k):
                    copy.start()

    copy_dinv.wait()
    copy_rhs.wait()
    unroll = max(u for u in range(1, 6) if leaves % u == 0)

    def over_leaves(body):
        def block(b, carry):
            for u in range(unroll):
                body(b * unroll + u)
            return carry
        lax.fori_loop(0, leaves // unroll, block, 0)

    def leaf_solve(i):
        fwd[i] = mm(dinv[i], rhs[i])

    over_leaves(leaf_solve)

    def leaf_term(k):
        copy_coup[k].wait()

        def block(b, acc):
            for u in range(unroll):
                i = b * unroll + u
                acc = acc + pat[k, i].astype(F32) * mm(coup[i, k], fwd[i])
            return acc

        terms[k] = lax.fori_loop(0, leaves // unroll, block, jnp.zeros(terms.shape[1:], F32))

    def flip(i):
        fwd_t[i] = fwd[i].T

    for k in reversed(range(depth)):
        leaf_term(k)
        if k < hub_level:

            @pl.when(owner(k))
            def _():
                terms[k] = terms[k] - trhs[0]

        @pl.when(odd)
        def _():
            part_copy(k).start()

    for level in reversed(range(hub_level)):

        @pl.when(jnp.logical_and(is_hub, me == entry(level)))
        def _():
            mat_wait(level)
            for k in reversed(range(level + 1)):
                for t, hub in others(level):
                    for copy in mat_parts(mats.at[level, k], level, k, t, hub):
                        copy.start()

    @pl.when(odd)
    def _():
        over_leaves(flip)

    @pl.when(even)
    def _():
        slot_wait(0, last)
        y = mm(tinv[0], trhs[0] - (terms[last] + slots[0, last]))
        for k in reversed(range(last)):
            slot_wait(0, k)
            stage[k] = terms[k] + slots[0, k] + mm(tcoup[0, k], y)

            @pl.when(left)
            def _():
                up_copy(0, k).start()

            @pl.when(jnp.logical_not(left))
            def _():
                up_copy(1, k).start()

        y_t[...] = y.T
        over_leaves(flip)

    @pl.when(is_hub)
    def _():
        def rest(k):
            slot_wait(0, k)
            slot_wait(1, k)
            return slots[0, k] + slots[1, k]

        y = mm(tinv[0], trhs[0] - rest(hub_level))
        top = hub_level - 1
        for k in reversed(range(hub_level)):
            mine[top, k] = rest(k) + mm(tcoup[0, k], y)
            swap_copy(top, k).start()
        y_t[...] = y.T
        for level in reversed(range(hub_level)):
            @pl.when(me != entry(level))
            def _():
                mat_wait(level)

            swap_copy(level, level).wait_recv()
            y = mm(mats[level, level], -(mine[level, level] + theirs[level, level]))
            for k in reversed(range(level)):
                swap_copy(level, k).wait_recv()
                mine[level - 1, k] = mine[level, k] + theirs[level, k] + mm(mats[level, k], y)
                swap_copy(level - 1, k).start()
            high_y[level] = y.T

        for level in range(hub_level + 1):
            own = level == hub_level
            value = y_t[...] if own else high_y[level]
            for k in range(level):
                value = value - mm(high_x[k], tcoup[0, k] if own else mats[level, k])
            high_x[level] = mm(value, tinv[0] if own else mats[level, level])
            down_copy(high_x.at[level], 1, level, me + 1).start()
            down_copy(high_x.at[level], 0, level, me - 1).start()
        top_out[0] = high_x[hub_level].T

    def leaf_back(k):
        x = path[k].astype(BF16)

        def body(i):
            value = fwd_t[i] - pat[k, i].astype(F32) * mm(x, coup[i, k])
            if k < last:
                fwd_t[i] = value
            else:
                out[i] = mm(value, dinv[i]).T
                pltpu.make_async_copy(out.at[i], sol_hbm.at[i], out_sem.at[i]).start()

        over_leaves(body)

    @pl.when(even)
    def _():
        for k in range(last):
            path_wait(k)
            pair_copy(k).start()
            y_t[...] = y_t[...] - mm(path[k], tcoup[0, k])
            if k + 1 == last:
                path[last] = mm(y_t[...], tinv[0])
                pair_copy(last).start()
            leaf_back(k)
        top_out[0] = path[last].T

    @pl.when(odd)
    def _():
        for k in range(last):
            path_wait(k)
            leaf_back(k)
        path_wait(last)

    for level in range(hub_level):

        @pl.when(owner(level))
        def _():
            top_out[0] = path[level].T

    @pl.when(me == (1 << depth) - 1)
    def _():
        top_out[0] = path[0].T

    copy_top = pltpu.make_async_copy(top_out, top_hbm, top_sem)
    copy_top.start()
    leaf_back(last)

    @pl.when(odd)
    def _():
        for k in range(depth):
            part_copy(k).wait_send()

    @pl.when(even)
    def _():
        for k in range(last):
            up_copy(0, k).wait_send()
        for k in range(depth):
            pair_copy(k).wait_send()

    @pl.when(is_hub)
    def _():
        for level in range(hub_level):
            for k in range(level + 1):
                swap_copy(level, k).wait_send()
        for k in range(hub_level + 1):
            down_copy(high_x.at[k], 0, k, partner).wait_send()
            down_copy(high_x.at[k], 1, k, partner).wait_send()

    for level in range(hub_level):

        @pl.when(owner(level))
        def _():
            for k in range(level + 1):
                for copy in own_parts(level, k):
                    copy.wait_send()

        @pl.when(jnp.logical_and(is_hub, me == entry(level)))
        def _():
            for k in range(level + 1):
                for t, hub in others(level):
                    for copy in mat_parts(mats.at[level, k], level, k, t, hub):
                        copy.wait_send()

    copy_top.wait()

    def out_wait(i):
        pltpu.make_async_copy(out.at[i], sol_hbm.at[i], out_sem.at[i]).wait()

    over_leaves(out_wait)


def local(leaf_right_hand, leaf_diagonal_inverse, leaf_coupling, leaf_pattern, top_rhs, top_inverse, top_coupling):
    depth = lax.axis_size("col").bit_length() - 1
    high = depth - 2
    leaves, width, right = leaf_right_hand.shape
    tall, flat = (width, right), (right, width)
    anywhere = pl.BlockSpec(memory_space=pl.ANY)
    sem = pltpu.SemaphoreType.DMA
    return pl.pallas_call(
        functools.partial(kernel, depth),
        out_shape=(
            jax.ShapeDtypeStruct(leaf_right_hand.shape, F32),
            jax.ShapeDtypeStruct(top_rhs.shape, F32),
        ),
        in_specs=[anywhere] * 3 + [pl.BlockSpec(memory_space=pltpu.SMEM)] + [anywhere] * 3,
        out_specs=(anywhere, anywhere),
        scratch_shapes=[
            pltpu.VMEM(leaf_right_hand.shape, F32),
            pltpu.VMEM(leaf_diagonal_inverse.shape, BF16),
            pltpu.VMEM(leaf_coupling.shape, BF16),
            pltpu.VMEM(top_rhs.shape, F32),
            pltpu.VMEM(top_inverse.shape, BF16),
            pltpu.VMEM(top_coupling.shape, BF16),
            pltpu.VMEM((leaves, *tall), F32),
            pltpu.VMEM((leaves, *flat), F32),
            pltpu.VMEM((leaves, *tall), F32),
            pltpu.VMEM((1, *tall), F32),
            pltpu.VMEM((depth, *tall), F32),
            pltpu.VMEM((2, depth, *tall), F32),
            pltpu.VMEM((depth, *tall), F32),
            pltpu.VMEM((depth, *flat), F32),
            pltpu.VMEM(flat, F32),
            pltpu.VMEM((high, width, width), F32),
            pltpu.VMEM((high, high, width, width), F32),
            pltpu.VMEM((high, high, *tall), F32),
            pltpu.VMEM((high, high, *tall), F32),
            pltpu.VMEM((high, *flat), F32),
            pltpu.VMEM((high + 1, *flat), F32),
            sem((2,)), sem((depth,)), sem((3,)), sem((leaves,)), sem,
            sem((2, depth)), sem((depth,)), sem((depth,)), sem((depth,)), sem((2, depth)),
            sem((high, 1 << high, high + 1)), sem((high, high)), sem((high,)), sem((high, high)), sem((high, high)),
        ],
        compiler_params=pltpu.CompilerParams(
            collective_id=0, has_side_effects=True, vmem_limit_bytes=56 * 2**20
        ),
    )(leaf_right_hand, leaf_diagonal_inverse, leaf_coupling, leaf_pattern.T, top_rhs, top_inverse, top_coupling)


def solution(mesh):
    both = ("grp", "col")
    three, four = P(both, None, None), P(both, None, None, None)
    in_specs = (three, three, four, P(both, None), three, three, four)
    return jax.shard_map(local, mesh=mesh, in_specs=in_specs, out_specs=(three, three), check_vma=False)
```
